256 devices in a mesh: inp: 4 (over z_lo), out: 8 (over x, core), row: 8 (over y, z_hi).
Axes of the slice: x: 4, y: 4, z: 8 (z_hi: 2, z_lo: 4; z = z_hi * 4 + z_lo), core: 2. Of those that a mesh axis runs over, the one named last changes fastest.
Arguments:
- inputs: bfloat16 [4096, 5120], P('row', 'inp'), may hold values from -6 to 6
- grad_out: bfloat16 [4096, 5120], P('row', 'inp'), may hold values from -6 to 6
- gate_in: bfloat16 [4096, 10240], P('row', 'out'), may hold values from -6 to 6
- up_in: bfloat16 [4096, 10240], P('row', 'out'), may hold values from -6 to 6
- gate_weight: bfloat16 [5120, 10240], P('inp', ('out', 'row')), may hold values from -0.078125 to 0.078125
- up_weight: bfloat16 [5120, 10240], P('inp', ('out', 'row')), may hold values from -0.078125 to 0.078125
- down_weight: bfloat16 [10240, 5120], P(('out', 'row'), 'inp'), may hold values from -0.0625 to 0.0625
Outputs:
- grad_inputs: bfloat16 [4096, 5120], P('row', 'inp')
- grad_gate_w: float32 [5120, 10240], P('inp', ('out', 'row'))
- grad_up_w: float32 [5120, 10240], P('inp', ('out', 'row'))
- grad_down_w: float32 [10240, 5120], P(('out', 'row'), 'inp')
The draws below stay inside these ranges and needn't reach their ends.
All inputs are finite; a program needn't handle non-finite values.
Results may differ from the reference program's by a relative error of at most 0.0049.
Values may be sent and summed in bfloat16 or wider, within the bound.
No kernel may reach another device: no remote copies, remote signals or barrier semaphores. Data moves between devices by JAX's collectives and lax.ppermute only.
A program may use at most 128 MiB of HBM per device.

```python
import jax
import jax.numpy as jnp

D = 5120
FF = 10240
TOKENS = 4096


def level_of(stream_key, dims, cuts, least, top_value):
    gain, own = 1.0, jax.random.fold_in(stream_key, 6)
    for axis_at, parts in cuts:
        draws = jnp.exp(jax.random.uniform(jax.random.fold_in(own, axis_at), (parts,), jnp.float32, least / len(cuts), top_value / len(cuts)))
        gain = gain * jnp.repeat(draws, dims[axis_at] // parts).reshape([-1 if axis == axis_at else 1 for axis in range(len(dims))])
    return gain


def bell_draw(rng, dims, width, reach, split=(), dtype=jnp.bfloat16):
    result = jax.random.normal(rng, dims, jnp.float32) * width
    if len(split) > 0:
        result = level_of(rng, dims, split, -0.22, 0.18) * result
    return jnp.clip(result, min=-reach, max=reach).astype(dtype)


def setup_inputs(seed: int = 0) -> dict:
    keys = jax.random.split(jax.random.key(seed), 8)
    inputs = bell_draw(keys[0], (TOKENS, D), 1.0, 6.0, ((0, 8), (1, 4)))
    grad_out = bell_draw(keys[1], (TOKENS, D), 1.0, 6.0, ((0, 8), (1, 4)))
    gate_in = bell_draw(keys[2], (TOKENS, FF), 1.5, 6.0, ((0, 8), (1, 8)))
    up_in = bell_draw(keys[3], (TOKENS, FF), 1.0, 6.0, ((0, 8), (1, 8)))
    gate_weight = bell_draw(keys[4], (D, FF), D ** -0.5, 0.078125, ((0, 4), (1, 64)))
    up_weight = bell_draw(keys[5], (D, FF), D ** -0.5, 0.078125, ((0, 4), (1, 64)))
    down_weight = bell_draw(keys[6], (FF, D), FF ** -0.5, 0.0625, ((0, 64), (1, 4)))
    return dict(inputs=inputs, grad_out=grad_out, gate_in=gate_in, up_in=up_in, gate_weight=gate_weight, up_weight=up_weight, down_weight=down_weight)


def reference(inputs, grad_out, gate_in, up_in, gate_weight, up_weight, down_weight):
    gate_values = gate_in.astype(jnp.float32)
    up_values = up_in.astype(jnp.float32)
    logistic = jax.nn.sigmoid(gate_values)
    activated = gate_values * logistic
    hidden = (activated * up_values).astype(jnp.bfloat16)
    grad_hidden = jnp.dot(grad_out, down_weight.T, preferred_element_type=jnp.float32)
    grad_gate = (grad_hidden * up_values * logistic * (1.0 + gate_values * (1.0 - logistic))).astype(jnp.bfloat16)
    grad_up = (grad_hidden * activated).astype(jnp.bfloat16)
    grad_down_w = jnp.dot(hidden.T, grad_out, preferred_element_type=jnp.float32)
    grad_gate_w = jnp.dot(inputs.T, grad_gate, preferred_element_type=jnp.float32)
    grad_up_w = jnp.dot(inputs.T, grad_up, preferred_element_type=jnp.float32)
    summed = jnp.dot(grad_gate, gate_weight.T, preferred_element_type=jnp.float32)
    summed = summed + jnp.dot(grad_up, up_weight.T, preferred_element_type=jnp.float32)
    return summed.astype(jnp.bfloat16), grad_gate_w, grad_up_w, grad_down_w
```

```python
import jax
import jax.numpy as jnp
from jax import lax
from jax.sharding import PartitionSpec as P

BF = jnp.bfloat16
F32 = jnp.float32


def on_device(inputs, grad_out, gate_in, up_in, gate_weight, up_weight, down_weight):
    x, c = lax.axis_index("out") // 2, lax.axis_index("out") % 2
    y, h = lax.axis_index("row") // 2, lax.axis_index("row") % 2
    l = lax.axis_index("inp")
    tokens, width = inputs.shape
    block = down_weight.shape[0]
    piece = tokens // 8

    def to_x(a, k):
        return lax.ppermute(a, "out", [(i, (i + 2 * k) % 8) for i in range(8)])

    def to_core(a):
        return lax.ppermute(a, "out", [(i, i ^ 1) for i in range(8)])

    def to_y(a, k):
        return lax.ppermute(a, "row", [(i, (i + 2 * k) % 8) for i in range(8)])

    def to_h(a):
        return lax.ppermute(a, "row", [(i, i ^ 1) for i in range(8)])

    def to_l(a, k):
        return lax.ppermute(a, "inp", [(i, (i + k) % 4) for i in range(4)])

    def rows(a, at, n):
        return lax.dynamic_slice_in_dim(a, at * n, n, 0)

    def gather(a, me, send):
        n = a.shape[0]
        got = jnp.zeros((4 * n,) + a.shape[1:], a.dtype)
        for k in range(4):
            part = a if k == 0 else send(a, k)
            got = lax.dynamic_update_slice_in_dim(got, part, ((me - k) % 4) * n, 0)
        return got

    def scatter(a, me, send):
        n = a.shape[0] // 4
        total = rows(a, me, n)
        for k in range(1, 4):
            total = total + send(rows(a, (me + k) % 4, n).astype(BF), k).astype(F32)
        return total

    def nt(a, b):
        return lax.dot_general(a, b, (((1,), (1,)), ((), ())), preferred_element_type=F32)

    def nn(a, b):
        return lax.dot_general(a, b, (((1,), (0,)), ((), ())), preferred_element_type=F32)

    def tn(a, b):
        return lax.dot_general(a, b, (((0,), (0,)), ((), ())), preferred_element_type=F32)

    def other_tokens(a):
        part = to_h(rows(a, 4 * c + x, piece))
        half = gather(part, x, to_x)
        swapped = to_core(half)
        return jnp.concatenate(
            [jnp.where(c == 0, half, swapped), jnp.where(c == 0, swapped, half)], 0
        )

    down = gather(down_weight, y, to_y)
    grad_out_b = other_tokens(grad_out)
    gate_t, up_t = gate_in.T, up_in.T

    def half_of(a, which):
        return lax.dynamic_index_in_dim(
            a.reshape(4, 2, block, tokens), which, 1, keepdims=False
        ).reshape(4 * block, tokens)

    gate_a, up_a = half_of(gate_t, h), half_of(up_t, h)
    at = 2 * l + 1 - h
    both = to_h(jnp.stack([rows(gate_t, at, block), rows(up_t, at, block)], 1).reshape(2 * block, tokens))
    both = gather(both, l, to_l).reshape(4, block, 2, tokens)
    gate_b, up_b = both[:, :, 0].reshape(-1, tokens), both[:, :, 1].reshape(-1, tokens)

    def hidden_grad(tok):
        own = scatter(nt(down, tok), l, to_l)
        return gather(own.astype(BF), l, to_l)

    gh_a = hidden_grad(grad_out)
    gh_b = hidden_grad(grad_out_b)
    inputs_b = other_tokens(inputs)
    weights = gather(
        jnp.concatenate([gate_weight.T, up_weight.T], 0), y, to_y
    ).reshape(4, 2, block, width)
    gate_w, up_w = weights[:, 0].reshape(-1, width), weights[:, 1].reshape(-1, width)

    def local(gh, gate, up):
        gh, gate, up = gh.astype(F32), gate.astype(F32), up.astype(F32)
        logistic = jax.nn.sigmoid(gate)
        activated = gate * logistic
        hidden = (activated * up).astype(BF)
        grad_gate = (gh * up * logistic * (1.0 + gate * (1.0 - logistic))).astype(BF)
        grad_up = (gh * activated).astype(BF)
        return hidden, grad_gate, grad_up

    hid_a, gg_a, gu_a = local(gh_a, gate_a, up_a)
    hid_b, gg_b, gu_b = local(gh_b, gate_b, up_b)

    grad_down_w = scatter(nn(hid_a, grad_out) + nn(hid_b, grad_out_b), y, to_y)

    part_b = tn(gg_b, gate_w) + tn(gu_b, up_w)
    part_a = tn(gg_a, gate_w) + tn(gu_a, up_w)
    part = jnp.stack([part_a, part_b], 0).reshape(2, 2, tokens // 2, width)
    keep = lax.dynamic_index_in_dim(part, c, 1, keepdims=False)
    give = lax.dynamic_index_in_dim(part, 1 - c, 1, keepdims=False)
    summed = keep + to_core(give)
    quarters = summed.reshape(2, 4, piece, width).transpose(1, 0, 2, 3).reshape(8 * piece, width)
    mine = scatter(quarters, x, to_x)
    mine = mine[:piece] + to_h(mine[piece:].astype(BF)).astype(F32)
    half = gather(mine.astype(BF), x, to_x)
    swapped = to_core(half)
    grad_inputs = jnp.concatenate(
        [jnp.where(c == 0, half, swapped), jnp.where(c == 0, swapped, half)], 0
    )

    grad_gate_w = scatter(nn(gg_a, inputs) + nn(gg_b, inputs_b), y, to_y).T
    grad_up_w = scatter(nn(gu_a, inputs) + nn(gu_b, inputs_b), y, to_y).T
    return (grad_inputs, grad_gate_w, grad_up_w, grad_down_w)


def solution(mesh):
    in_specs = (
        P("row", "inp"),
        P("row", "inp"),
        P("row", "out"),
        P("row", "out"),
        P("inp", ("out", "row")),
        P("inp", ("out", "row")),
        P(("out", "row"), "inp"),
    )
    out_specs = (
        P("row", "inp"),
        P("inp", ("out", "row")),
        P("inp", ("out", "row")),
        P(("out", "row"), "inp"),
    )
    return jax.shard_map(
        on_device, mesh=mesh, in_specs=in_specs, out_specs=out_specs, check_vma=False
    )
```

```python
import jax
import jax.numpy as jnp
from jax import lax
from jax.sharding import Mesh, PartitionSpec as P

BF = jnp.bfloat16
F32 = jnp.float32


def after(a, *earlier):
    return lax.optimization_barrier((a,) + earlier)[0]


def send(a, axis, k, n=4):
    return lax.ppermute(a, axis, [(i, (i + k) % n) for i in range(n)])


def swap(a, axis):
    return send(a, axis, 1, 2)


def rows(a, at, n):
    return lax.dynamic_slice_in_dim(a, at * n, n, 0)


def nt(a, b):
    return lax.dot_general(a, b, (((1,), (1,)), ((), ())), preferred_element_type=F32)


def nn(a, b):
    return lax.dot_general(a, b, (((1,), (0,)), ((), ())), preferred_element_type=F32)


def tn(a, b):
    return lax.dot_general(a, b, (((0,), (0,)), ((), ())), preferred_element_type=F32)


def to_all(a, axis):
    return lax.all_to_all(jnp.tile(a, (4, 1)), axis, 0, 0, tiled=True)


def pick(a, at):
    return lax.dynamic_index_in_dim(a, at, 0, keepdims=False)


def place(parts, me):
    n = len(parts)
    slot = lax.broadcasted_iota(jnp.int32, (n, 1, 1), 0)
    got = parts[0][None]
    for k in range(1, n):
        got = jnp.where(slot == (me + k) % n, parts[k][None], got)
    return got


def place_xor(parts, me):
    slot = lax.broadcasted_iota(jnp.int32, (4, 1, 1), 0)
    got = parts[3][None]
    for k, part in zip((0, 2, 1), parts):
        got = jnp.where(slot == (me ^ k), part[None], got)
    return got


def from_all(a, axis):
    return [a] + [send(a, axis, -k) for k in (1, 2, 3)]


def fence(*values):
    return lax.optimization_barrier(values)


def exchange(a, k):
    return lax.ppermute(a, "inp", [(i, i ^ k) for i in range(4)])


def on_device(inputs, grad_out, gate_in, up_in, gate_weight, up_weight, down_weight):
    x, c, y, h = (lax.axis_index(name) for name in ("x", "core", "y", "h"))
    l = lax.axis_index("inp")
    tokens, width = inputs.shape
    block = down_weight.shape[0]
    piece = tokens // 8
    half = tokens // 2

    def in_order(part, swapped):
        part, swapped = part.reshape(half, width), swapped.reshape(half, width)
        return place([part, swapped], c).reshape(tokens, width)

    def half_of(a, which):
        a = a.T.reshape(4, 2, block, -1)
        return lax.dynamic_index_in_dim(a, which, 1, keepdims=False)

    both = jnp.concatenate(
        [rows(grad_out, 4 * c + x, piece), rows(inputs, 4 * c + x, piece)], 0
    )
    both, down_weight = fence(both, down_weight)
    both = swap(both, "h")
    down = to_all(down_weight, "y").reshape(4, block, width)
    ends = lax.optimization_barrier(jnp.where(l == 3, gate_in, up_in))
    ends = half_of(ends, 1 - h)
    both, ends, gate_in, up_in, gate_weight, up_weight = fence(
        both, ends, gate_in, up_in, gate_weight, up_weight
    )
    g_piece, x_piece = both[:piece], both[piece:]
    ends = lax.ppermute(ends, ("inp", "h"), [(6, 1), (7, 0), (0, 7), (1, 6)])
    parts = from_all(g_piece, "x")
    both_w = jnp.concatenate([gate_weight.T, up_weight.T], 0)
    *parts, down, both_w, gate_in, up_in = fence(*parts, down, both_w, gate_in, up_in)

    weights = lax.all_gather(both_w, "y", axis=0, tiled=True)
    down_keep = jnp.concatenate([pick(down, l), pick(down, l ^ 2)], 0)
    down_give = jnp.concatenate([pick(down, l ^ 1), pick(down, l ^ 3)], 0)

    def terms_of(tok):
        return nt(down_keep, tok), nt(down_give, tok).astype(BF)

    def pair(keep, got):
        both = keep + got.astype(F32)
        return both[:block], both[block:].astype(BF)

    def whole(mine, got, others):
        return place_xor([mine, got, others[:block], others[block:]], l)

    mine_x = place(parts, x)
    grad_out_b = in_order(mine_x, swap(mine_x, "core"))
    keep_a, give_a = terms_of(grad_out)
    got_a = exchange(give_a, 1)
    near = lax.ppermute(ends, "inp", [(0, 1), (3, 2)])
    keep_b, give_b = terms_of(grad_out_b)
    mine_a, give_a = pair(keep_a, got_a)
    mine_a, give_a, near, keep_b, give_b, gate_in, up_in, x_piece = fence(
        mine_a, give_a, near, keep_b, give_b, gate_in, up_in, x_piece
    )

    got_a = exchange(give_a, 2)
    got_b = exchange(give_b, 1)
    far = lax.ppermute(near, "inp", [(1, 2), (2, 1)])
    mine_x = to_all(x_piece, "x")
    gate_a, up_a = half_of(gate_in, h), half_of(up_in, h)
    mine_a = (mine_a + got_a.astype(F32)).astype(BF)
    mine_b, give_b = pair(keep_b, got_b)
    mine_a, mine_b, give_b, far, gate_a, up_a, mine_x = fence(
        mine_a, mine_b, give_b, far, gate_a, up_a, mine_x
    )

    got_a = exchange(mine_a, 2)
    got_b = exchange(give_b, 2)
    last = lax.ppermute(far, "inp", [(2, 3), (1, 0)])
    inputs_b = in_order(mine_x, swap(mine_x, "core"))
    mine_b = (mine_b + got_b.astype(F32)).astype(BF)
    both_a = jnp.concatenate([mine_a, got_a], 0)
    both_a, mine_b, last, inputs_b = fence(both_a, mine_b, last, inputs_b)

    gate_b = jnp.where(l == 0, ends, jnp.where(l == 1, near, jnp.where(l == 2, far, last)))
    up_b = jnp.where(l == 3, ends, jnp.where(l == 2, near, jnp.where(l == 1, far, last)))
    others_a = exchange(both_a, 1)
    got_b = exchange(mine_b, 2)

    def gate_part(gate, up):
        gate, up = gate.astype(F32), up.astype(F32)
        logistic = jax.nn.sigmoid(gate)
        activated = gate * logistic
        return (activated * up).astype(BF).reshape(4 * block, tokens)

    def grad_part(gh, gate, up):
        gh, gate, up = gh.astype(F32), gate.astype(F32), up.astype(F32)
        logistic = jax.nn.sigmoid(gate)
        grad_gate = (gh * up * logistic * (1.0 + gate * (1.0 - logistic))).astype(BF)
        grad_up = (gh * (gate * logistic)).astype(BF)
        return jnp.stack([grad_gate, grad_up], 1).reshape(8 * block, tokens)

    def terms_y(left, right):
        n = left.shape[0] // 4
        terms = [nn(rows(left, (y + k) % 4, n), right) for k in range(4)]
        return terms[0], [a.astype(BF) for a in terms[1:]]

    def add(own, got):
        for a in got:
            own = own + a.astype(F32)
        return own

    both_b = jnp.concatenate([mine_b, got_b], 0)
    others_a, both_b = fence(others_a, both_b)

    def over_core(a):
        return (rows(a, c, half) + swap(rows(a, 1 - c, half), "core")).reshape(4, piece, width)

    others_b = exchange(both_b, 1)
    hidden = jnp.concatenate([gate_part(gate_a, up_a), gate_part(gate_b, up_b)], 1)
    down_terms = nn(hidden, jnp.concatenate([grad_out, grad_out_b], 0)).astype(BF)
    grad_down_w = lax.psum_scatter(down_terms, "y", scatter_dimension=0, tiled=True)
    grads_a = grad_part(whole(both_a[:block], both_a[block:], others_a), gate_a, up_a)
    sum_a = tn(grads_a, weights)
    others_b, sum_a, down_terms = fence(others_b, sum_a, down_terms)

    grads_b = grad_part(whole(both_b[:block], both_b[block:], others_b), gate_b, up_b)
    core_a = over_core(sum_a)
    core_b = over_core(tn(grads_b, weights))
    left = jnp.concatenate([grads_a, grads_b], 1)
    right = jnp.concatenate([inputs, inputs_b], 0)

    def term_w(k):
        return nn(rows(left, (y + k) % 4, 2 * block), right)

    term_1, term_3 = term_w(1).astype(BF), term_w(3).astype(BF)
    core_a, core_b, term_1, term_3 = fence(core_a, core_b, term_1, term_3)

    got_1, got_3 = send(term_1, "y", 1), send(term_3, "y", 3)
    core = jnp.stack([core_a, core_b], 1)
    got = lax.all_to_all(core.astype(BF), "x", 0, 0, tiled=True).astype(F32)
    slot = lax.broadcasted_iota(jnp.int32, (4, 1, 1, 1), 0)
    summed = pick(core, x) + jnp.sum(jnp.where(slot == x, 0.0, got), axis=0)
    term_2 = term_w(2).astype(BF)
    summed, got_1, got_3, term_2 = fence(summed, got_1, got_3, term_2)

    got_2 = send(term_2, "y", 2)
    summed = summed[0] + swap(summed[1].astype(BF), "h").astype(F32)
    out_mine = to_all(summed.astype(BF), "x")
    out_theirs = swap(out_mine, "core")
    out_theirs, got_2 = fence(out_theirs, got_2)
    grad_inputs = in_order(out_mine, out_theirs)

    grad_w = term_w(0)
    for a in (got_1, got_3, got_2):
        grad_w = grad_w + a.astype(F32)
    return (grad_inputs, grad_w[:block].T, grad_w[block:].T, grad_down_w.astype(F32))


def solution(mesh):
    fine = Mesh(mesh.devices.reshape(4, 4, 2, 4, 2), ("inp", "x", "core", "y", "h"))
    out, row = ("x", "core"), ("y", "h")
    in_specs = (
        P(row, "inp"),
        P(row, "inp"),
        P(row, out),
        P(row, out),
        P("inp", out + row),
        P("inp", out + row),
        P(out + row, "inp"),
    )
    out_specs = (
        P(row, "inp"),
        P("inp", out + row),
        P("inp", out + row),
        P(out + row, "inp"),
    )
    return jax.shard_map(
        on_device, mesh=fine, in_specs=in_specs, out_specs=out_specs, check_vma=False
    )
```

```python
import jax
import jax.numpy as jnp
from jax import lax
from jax.sharding import Mesh, PartitionSpec as P

BF = jnp.bfloat16
F32 = jnp.float32


def after(a, *earlier):
    return lax.optimization_barrier((a,) + earlier)[0]


def send(a, axis, k, n=4):
    return lax.ppermute(a, axis, [(i, (i + k) % n) for i in range(n)])


def swap(a, axis):
    return send(a, axis, 1, 2)


def rows(a, at, n):
    return lax.dynamic_slice_in_dim(a, at * n, n, 0)


def nt(a, b):
    return lax.dot_general(a, b, (((1,), (1,)), ((), ())), preferred_element_type=F32)


def nn(a, b):
    return lax.dot_general(a, b, (((1,), (0,)), ((), ())), preferred_element_type=F32)


def tn(a, b):
    return lax.dot_general(a, b, (((0,), (0,)), ((), ())), preferred_element_type=F32)


def to_all(a, axis):
    return lax.all_to_all(jnp.tile(a, (4, 1)), axis, 0, 0, tiled=True)


def pick(a, at):
    return lax.dynamic_index_in_dim(a, at, 0, keepdims=False)


def place(parts, me):
    n = len(parts)
    slot = lax.broadcasted_iota(jnp.int32, (n, 1, 1), 0)
    got = parts[0][None]
    for k in range(1, n):
        got = jnp.where(slot == (me + k) % n, parts[k][None], got)
    return got


def place_xor(parts, me):
    slot = lax.broadcasted_iota(jnp.int32, (4, 1, 1), 0)
    got = parts[3][None]
    for k, part in zip((0, 2, 1), parts):
        got = jnp.where(slot == (me ^ k), part[None], got)
    return got


def from_all(a, axis):
    return [a] + [send(a, axis, -k) for k in (1, 2, 3)]


def fence(*values):
    return lax.optimization_barrier(values)


def exchange(a, k, axis="inp"):
    return lax.ppermute(a, axis, [(i, i ^ k) for i in range(4)])


def on_device(inputs, grad_out, gate_in, up_in, gate_weight, up_weight, down_weight):
    x, c, y, h = (lax.axis_index(name) for name in ("x", "core", "y", "h"))
    l = lax.axis_index("inp")
    tokens, width = inputs.shape
    block = down_weight.shape[0]
    piece = tokens // 8
    half = tokens // 2

    def in_order(part, swapped):
        part, swapped = part.reshape(half, width), swapped.reshape(half, width)
        return place([part, swapped], c).reshape(tokens, width)

    def half_of(a, which):
        a = a.T.reshape(4, 2, block, -1)
        return lax.dynamic_index_in_dim(a, which, 1, keepdims=False)

    both = jnp.concatenate(
        [rows(grad_out, 4 * c + x, piece), rows(inputs, 4 * c + x, piece)], 0
    )
    both = swap(both, "h")
    down = lax.all_gather(down_weight, "y", axis=0)
    ends = lax.cond(
        l == 3, lambda g, u: half_of(g, 1 - h), lambda g, u: half_of(u, 1 - h), gate_in, up_in
    )
    both, ends, gate_in, up_in, gate_weight, up_weight = fence(
        both, ends, gate_in, up_in, gate_weight, up_weight
    )
    g_piece, x_piece = both[:piece], both[piece:]
    ends = lax.ppermute(ends, ("inp", "h"), [(6, 1), (7, 0), (0, 7), (1, 6)])
    parts = from_all(g_piece, "x")
    both_w = jnp.concatenate([gate_weight.T, up_weight.T], 0)
    *parts, down, both_w, gate_in, up_in = fence(*parts, down, both_w, gate_in, up_in)

    weights = lax.all_gather(both_w, "y", axis=0, tiled=True)
    x_all = lax.all_gather(x_piece, ("x", "core"), axis=0, tiled=True)
    down_keep = jnp.concatenate([pick(down, l), pick(down, l ^ 2)], 0)
    down_give = jnp.concatenate([pick(down, l ^ 1), pick(down, l ^ 3)], 0)

    def terms_of(tok):
        return nt(down_keep, tok), nt(down_give, tok).astype(BF)

    def pair(keep, got):
        both = keep + got.astype(F32)
        return both[:block], both[block:].astype(BF)

    def whole(mine, got, others):
        return place_xor([mine, got, others[:block], others[block:]], l)

    mine_x = place(parts, x)
    grad_out_b = in_order(mine_x, swap(mine_x, "core"))
    keep_a, give_a = terms_of(grad_out)
    got_a = exchange(give_a, 1)
    near = lax.ppermute(ends, "inp", [(0, 1), (3, 2)])
    keep_b, give_b = terms_of(grad_out_b)
    mine_a, give_a = pair(keep_a, got_a)
    mine_a, give_a, near, keep_b, give_b, gate_in, up_in = fence(
        mine_a, give_a, near, keep_b, give_b, gate_in, up_in
    )

    got_a = exchange(give_a, 2)
    got_b = exchange(give_b, 1)
    far = lax.ppermute(near, "inp", [(1, 2), (2, 1)])
    gate_a, up_a = half_of(gate_in, h), half_of(up_in, h)
    mine_a = (mine_a + got_a.astype(F32)).astype(BF)
    mine_b, give_b = pair(keep_b, got_b)
    mine_a, mine_b, give_b, far, gate_a, up_a = fence(mine_a, mine_b, give_b, far, gate_a, up_a)

    got_a = exchange(mine_a, 2)
    got_b = exchange(give_b, 2)
    last = lax.ppermute(far, "inp", [(2, 3), (1, 0)])
    mine_b = (mine_b + got_b.astype(F32)).astype(BF)
    both_a = jnp.concatenate([mine_a, got_a], 0)
    both_a, mine_b, last, x_all = fence(both_a, mine_b, last, x_all)

    gate_b = jnp.where(l == 0, ends, jnp.where(l == 1, near, jnp.where(l == 2, far, last)))
    up_b = jnp.where(l == 3, ends, jnp.where(l == 2, near, jnp.where(l == 1, far, last)))
    others_a = exchange(both_a, 1)
    got_b = exchange(mine_b, 2)

    def gate_part(gate, up):
        gate, up = gate.astype(F32), up.astype(F32)
        logistic = jax.nn.sigmoid(gate)
        activated = gate * logistic
        return (activated * up).astype(BF).reshape(4 * block, tokens)

    def grad_part(gh, gate, up):
        gh, gate, up = gh.astype(F32), gate.astype(F32), up.astype(F32)
        logistic = jax.nn.sigmoid(gate)
        grad_gate = (gh * up * logistic * (1.0 + gate * (1.0 - logistic))).astype(BF)
        grad_up = (gh * (gate * logistic)).astype(BF)
        return jnp.stack([grad_gate, grad_up], 1).reshape(8 * block, tokens)

    def terms_y(left, right):
        n = left.shape[0] // 4
        terms = [nn(rows(left, (y + k) % 4, n), right) for k in range(4)]
        return terms[0], [a.astype(BF) for a in terms[1:]]

    def add(own, got):
        for a in got:
            own = own + a.astype(F32)
        return own

    both_b = jnp.concatenate([mine_b, got_b], 0)
    inputs_b = x_all.reshape(4, 2, piece, width).transpose(1, 0, 2, 3).reshape(tokens, width)
    hidden = jnp.concatenate([gate_part(gate_a, up_a), gate_part(gate_b, up_b)], 1)
    down_terms = nn(hidden, jnp.concatenate([grad_out, grad_out_b], 0)).astype(BF)
    others_a, both_b, inputs_b, down_terms = fence(others_a, both_b, inputs_b, down_terms)
    grad_down_w = lax.psum_scatter(down_terms, "y", scatter_dimension=0, tiled=True)

    def over_core(a):
        return (rows(a, c, half) + swap(rows(a, 1 - c, half), "core")).reshape(4, piece, width)

    others_b = exchange(both_b, 1)
    grads_a = grad_part(whole(both_a[:block], both_a[block:], others_a), gate_a, up_a)
    sum_a = tn(grads_a, weights)
    others_b, sum_a = fence(others_b, sum_a)

    grads_b = grad_part(whole(both_b[:block], both_b[block:], others_b), gate_b, up_b)
    core_a = over_core(sum_a)
    sum_b = tn(grads_b, weights)
    grads_a, grads_b, sum_b = fence(grads_a, grads_b, sum_b)
    core_b = over_core(sum_b)
    left = jnp.concatenate([grads_a, grads_b], 1)
    right = jnp.concatenate([inputs, inputs_b], 0)

    def term_w(k):
        return nn(rows(left, (y + k) % 4, 2 * block), right)

    cols = width // 2
    term_2 = term_w(2).astype(BF)
    up_half, down_half = send(term_2[:, :cols], "y", 1), send(term_2[:, cols:], "y", 3)
    term_1, term_3 = fence(term_w(1), term_w(3))
    core_a, core_b, term_1, term_3 = fence(core_a, core_b, term_1, term_3)

    none = jnp.zeros_like(up_half)
    term_1 = term_1 + jnp.concatenate([up_half, none], 1).astype(F32)
    term_3 = term_3 + jnp.concatenate([none, down_half], 1).astype(F32)
    got_1, got_3 = send(term_1.astype(BF), "y", 1), send(term_3.astype(BF), "y", 3)
    core = jnp.stack([core_a, core_b], 1)
    got = lax.all_to_all(core.astype(BF), "x", 0, 0, tiled=True).astype(F32)
    slot = lax.broadcasted_iota(jnp.int32, (4, 1, 1, 1), 0)
    summed = pick(core, x) + jnp.sum(jnp.where(slot == x, 0.0, got), axis=0)
    theirs = swap(summed[1].astype(BF), "h")
    theirs, got_1, got_3, grad_down_w = fence(theirs, got_1, got_3, grad_down_w)
    out_mine = to_all((summed[0] + theirs.astype(F32)).astype(BF), "x")
    grad_w = term_w(0) + got_1.astype(F32) + got_3.astype(F32)
    out_mine, grad_w = fence(out_mine, grad_w)
    grad_inputs = in_order(out_mine, swap(out_mine, "core"))
    return (grad_inputs, grad_w[:block].T, grad_w[block:].T, grad_down_w.astype(F32))


def solution(mesh):
    fine = Mesh(mesh.devices.reshape(4, 4, 2, 4, 2), ("inp", "x", "core", "y", "h"))
    out, row = ("x", "core"), ("y", "h")
    in_specs = (
        P(row, "inp"),
        P(row, "inp"),
        P(row, out),
        P(row, out),
        P("inp", out + row),
        P("inp", out + row),
        P(out + row, "inp"),
    )
    out_specs = (
        P(row, "inp"),
        P("inp", out + row),
        P("inp", out + row),
        P(out + row, "inp"),
    )
    return jax.shard_map(
        on_device, mesh=fine, in_specs=in_specs, out_specs=out_specs, check_vma=False
    )
```

```python
import jax
import jax.numpy as jnp
from jax import lax
from jax.sharding import Mesh, PartitionSpec as P

BF = jnp.bfloat16
F32 = jnp.float32


def after(a, *earlier):
    return lax.optimization_barrier((a,) + earlier)[0]


def send(a, axis, k, n=4):
    return lax.ppermute(a, axis, [(i, (i + k) % n) for i in range(n)])


def swap(a, axis):
    return send(a, axis, 1, 2)


def rows(a, at, n):
    return lax.dynamic_slice_in_dim(a, at * n, n, 0)


def nt(a, b):
    return lax.dot_general(a, b, (((1,), (1,)), ((), ())), preferred_element_type=F32)


def nn(a, b):
    return lax.dot_general(a, b, (((1,), (0,)), ((), ())), preferred_element_type=F32)


def tn(a, b):
    return lax.dot_general(a, b, (((0,), (0,)), ((), ())), preferred_element_type=F32)


def to_all(a, axis):
    return lax.all_to_all(jnp.tile(a, (4, 1)), axis, 0, 0, tiled=True)


def pick(a, at):
    return lax.dynamic_index_in_dim(a, at, 0, keepdims=False)


def place(parts, me):
    n = len(parts)
    slot = lax.broadcasted_iota(jnp.int32, (n, 1, 1), 0)
    got = parts[0][None]
    for k in range(1, n):
        got = jnp.where(slot == (me + k) % n, parts[k][None], got)
    return got


def place_xor(parts, me):
    slot = lax.broadcasted_iota(jnp.int32, (4, 1, 1), 0)
    got = parts[3][None]
    for k, part in zip((0, 2, 1), parts):
        got = jnp.where(slot == (me ^ k), part[None], got)
    return got


def from_all(a, axis):
    return [a] + [send(a, axis, -k) for k in (1, 2, 3)]


def fence(*values):
    return lax.optimization_barrier(values)


def exchange(a, k, axis="inp"):
    return lax.ppermute(a, axis, [(i, i ^ k) for i in range(4)])


def on_device(inputs, grad_out, gate_in, up_in, gate_weight, up_weight, down_weight):
    x, c, y, h = (lax.axis_index(name) for name in ("x", "core", "y", "h"))
    l = lax.axis_index("inp")
    tokens, width = inputs.shape
    block = down_weight.shape[0]
    piece = tokens // 8
    half = tokens // 2

    def in_order(part, swapped):
        part, swapped = part.reshape(half, width), swapped.reshape(half, width)
        return place([part, swapped], c).reshape(tokens, width)

    def half_of(a, which):
        a = a.T.reshape(4, 2, block, -1)
        return lax.dynamic_index_in_dim(a, which, 1, keepdims=False)

    both = jnp.concatenate(
        [rows(grad_out, 4 * c + x, piece), rows(inputs, 4 * c + x, piece)], 0
    )
    both = swap(both, "h")
    down = lax.all_gather(down_weight, "y", axis=0)
    ends = lax.cond(
        l == 3, lambda g, u: half_of(g, 1 - h), lambda g, u: half_of(u, 1 - h), gate_in, up_in
    )
    both, ends, gate_in, up_in, gate_weight, up_weight = fence(
        both, ends, gate_in, up_in, gate_weight, up_weight
    )
    g_piece, x_piece = both[:piece], both[piece:]
    ends = lax.ppermute(ends, ("inp", "h"), [(6, 1), (7, 0), (0, 7), (1, 6)])
    parts = from_all(g_piece, "x")
    both_w = jnp.concatenate([gate_weight.T, up_weight.T], 0)
    *parts, down, both_w, gate_in, up_in = fence(*parts, down, both_w, gate_in, up_in)

    weights = lax.all_gather(both_w, "y", axis=0, tiled=True)
    inputs_b = lax.all_gather(x_piece, ("core", "x"), axis=0, tiled=True)
    down_keep = jnp.concatenate([pick(down, l), pick(down, l ^ 2)], 0)
    down_give = jnp.concatenate([pick(down, l ^ 1), pick(down, l ^ 3)], 0)

    def terms_of(tok):
        return nt(down_keep, tok), nt(down_give, tok).astype(BF)

    def pair(keep, got):
        both = keep + got.astype(F32)
        return both[:block], both[block:].astype(BF)

    def whole(mine, got, others):
        return place_xor([mine, got, others[:block], others[block:]], l)

    mine_x = place(parts, x)
    grad_out_b = in_order(mine_x, swap(mine_x, "core"))
    keep_a, give_a = terms_of(grad_out)
    got_a = exchange(give_a, 1)
    near = lax.ppermute(ends, "inp", [(0, 1), (3, 2)])
    keep_b, give_b = terms_of(grad_out_b)
    mine_a, give_a = pair(keep_a, got_a)
    mine_a, give_a, near, keep_b, give_b, gate_in, up_in = fence(
        mine_a, give_a, near, keep_b, give_b, gate_in, up_in
    )

    got_a = exchange(give_a, 2)
    got_b = exchange(give_b, 1)
    far = lax.ppermute(near, "inp", [(1, 2), (2, 1)])
    gate_a, up_a = half_of(gate_in, h), half_of(up_in, h)
    mine_a = (mine_a + got_a.astype(F32)).astype(BF)
    mine_b, give_b = pair(keep_b, got_b)
    mine_a, mine_b, give_b, far, gate_a, up_a = fence(mine_a, mine_b, give_b, far, gate_a, up_a)

    got_a = exchange(mine_a, 2)
    got_b = exchange(give_b, 2)
    last = lax.ppermute(far, "inp", [(2, 3), (1, 0)])
    mine_b = (mine_b + got_b.astype(F32)).astype(BF)
    both_a = jnp.concatenate([mine_a, got_a], 0)
    both_a, mine_b, last, inputs_b = fence(both_a, mine_b, last, inputs_b)

    gate_b = jnp.where(l == 0, ends, jnp.where(l == 1, near, jnp.where(l == 2, far, last)))
    up_b = jnp.where(l == 3, ends, jnp.where(l == 2, near, jnp.where(l == 1, far, last)))
    others_a = exchange(both_a, 1)
    got_b = exchange(mine_b, 2)

    def gate_part(gate, up):
        gate, up = gate.astype(F32), up.astype(F32)
        logistic = jax.nn.sigmoid(gate)
        activated = gate * logistic
        return (activated * up).astype(BF).reshape(4 * block, tokens)

    def grad_part(gh, gate, up):
        gh, gate, up = gh.astype(F32), gate.astype(F32), up.astype(F32)
        logistic = jax.nn.sigmoid(gate)
        grad_gate = (gh * up * logistic * (1.0 + gate * (1.0 - logistic))).astype(BF)
        grad_up = (gh * (gate * logistic)).astype(BF)
        return jnp.stack([grad_gate, grad_up], 1).reshape(8 * block, tokens)

    def terms_y(left, right):
        n = left.shape[0] // 4
        terms = [nn(rows(left, (y + k) % 4, n), right) for k in range(4)]
        return terms[0], [a.astype(BF) for a in terms[1:]]

    def add(own, got):
        for a in got:
            own = own + a.astype(F32)
        return own

    both_b = jnp.concatenate([mine_b, got_b], 0)
    hidden = jnp.concatenate([gate_part(gate_a, up_a), gate_part(gate_b, up_b)], 1)
    down_terms = nn(hidden, jnp.concatenate([grad_out, grad_out_b], 0)).astype(BF)
    others_a, both_b, down_terms = fence(others_a, both_b, down_terms)
    grad_down_w = lax.psum_scatter(down_terms, "y", scatter_dimension=0, tiled=True)

    def over_core(a):
        return (rows(a, c, half) + swap(rows(a, 1 - c, half), "core")).reshape(4, piece, width)

    others_b = exchange(both_b, 1)
    grads_a = grad_part(whole(both_a[:block], both_a[block:], others_a), gate_a, up_a)
    sum_a = tn(grads_a, weights)
    others_b, sum_a = fence(others_b, sum_a)

    grads_b = grad_part(whole(both_b[:block], both_b[block:], others_b), gate_b, up_b)
    core_a = over_core(sum_a)
    sum_b = tn(grads_b, weights)
    grads_a, grads_b, sum_b = fence(grads_a, grads_b, sum_b)
    core_b = over_core(sum_b)
    left = jnp.concatenate([grads_a, grads_b], 1)
    right = jnp.concatenate([inputs, inputs_b], 0)

    def term_w(k):
        return nn(rows(left, (y + k) % 4, 2 * block), right)

    cols = width // 2
    term_2 = term_w(2).astype(BF)
    up_half, down_half = send(term_2[:, :cols], "y", 1), send(term_2[:, cols:], "y", 3)
    core_a, core_b, left, term_2 = fence(core_a, core_b, left, term_2)
    term_1, term_3 = fence(term_w(1), term_w(3))

    none = jnp.zeros_like(up_half)
    term_1 = term_1 + jnp.concatenate([up_half, none], 1).astype(F32)
    term_3 = term_3 + jnp.concatenate([none, down_half], 1).astype(F32)
    got_1, got_3 = send(term_1.astype(BF), "y", 1), send(term_3.astype(BF), "y", 3)
    core = jnp.stack([core_a, core_b], 1)
    got = lax.all_to_all(core.astype(BF), "x", 0, 0, tiled=True).astype(F32)
    slot = lax.broadcasted_iota(jnp.int32, (4, 1, 1, 1), 0)
    summed = pick(core, x) + jnp.sum(jnp.where(slot == x, 0.0, got), axis=0)
    theirs = swap(summed[1].astype(BF), "h")
    theirs, got_1, got_3, grad_down_w = fence(theirs, got_1, got_3, grad_down_w)
    out_mine = to_all((summed[0] + theirs.astype(F32)).astype(BF), "x")
    grad_w = term_w(0) + got_1.astype(F32) + got_3.astype(F32)
    out_mine, grad_w = fence(out_mine, grad_w)
    grad_inputs = in_order(out_mine, swap(out_mine, "core"))
    return (grad_inputs, grad_w[:block].T, grad_w[block:].T, grad_down_w.astype(F32))


def solution(mesh):
    fine = Mesh(mesh.devices.reshape(4, 4, 2, 4, 2), ("inp", "x", "core", "y", "h"))
    out, row = ("x", "core"), ("y", "h")
    in_specs = (
        P(row, "inp"),
        P(row, "inp"),
        P(row, out),
        P(row, out),
        P("inp", out + row),
        P("inp", out + row),
        P(out + row, "inp"),
    )
    out_specs = (
        P(row, "inp"),
        P("inp", out + row),
        P("inp", out + row),
        P(out + row, "inp"),
    )
    return jax.shard_map(
        on_device, mesh=fine, in_specs=in_specs, out_specs=out_specs, check_vma=False
    )
```
